512 devices in a mesh: clip: 16 (over z_hi, x), frame: 32 (over y, z_lo, core).
Axes of the slice: x: 4, y: 8, z: 8 (z_hi: 4, z_lo: 2; z = z_hi * 2 + z_lo), core: 2. Of those that a mesh axis runs over, the one named last changes fastest.
Arguments:
- queries: bfloat16 [16, 32, 256, 1152], P('clip', 'frame'), may hold values from -16 to 16
- keys: bfloat16 [16, 32, 256, 1152], P('clip', 'frame'), may hold values from -16 to 16
- values: bfloat16 [16, 32, 256, 1152], P('clip', 'frame'), may hold values from -6 to 6
- grad_out: bfloat16 [16, 32, 256, 1152], P('clip', 'frame'), may hold values from -6 to 6
- w_out: bfloat16 [1152, 1152], P('frame'), may hold values from -0.1875 to 0.1875
Outputs:
- grad_queries: bfloat16 [16, 32, 256, 1152], P('clip', 'frame')
- grad_keys: bfloat16 [16, 32, 256, 1152], P('clip', 'frame')
- grad_values: bfloat16 [16, 32, 256, 1152], P('clip', 'frame')
- grad_weight: float32 [1152, 1152], P('frame')
The draws below stay inside these ranges and needn't reach their ends.
All inputs are finite; a program needn't handle non-finite values.
Results may differ from the reference program's by a relative error of at most 0.0058.
Values may be sent and summed in bfloat16 or wider, within the bound.
No kernel may reach another device: no remote copies, remote signals or barrier semaphores. Data moves between devices by JAX's collectives and lax.ppermute only.
A program may use at most 64 MiB of HBM per device.

```python
import jax
import jax.numpy as jnp
from jax import lax

D = 1152
HEADS = 16
S = 256
HEAD_DIM = 72
F = 32
CLIPS = 16


def draw_queries(key, part):
    key = jax.random.fold_in(key, 11)
    own = jax.random.truncated_normal(key, -4.0, 4.0, (CLIPS, F, S, D), jnp.float32)
    return own.astype(jnp.bfloat16)


def draw_keys(key, part):
    key = jax.random.fold_in(key, 23)
    own = jax.random.truncated_normal(key, -4.0, 4.0, (CLIPS, F, S, D), jnp.float32)
    return own.astype(jnp.bfloat16)


def shard_levels(own_key, dims, cuts, low, high):
    def one(position, parts):
        steps = jax.random.uniform(jax.random.fold_in(jax.random.fold_in(own_key, 6), position), (parts,), jnp.float32, low / len(cuts), high / len(cuts))
        return jnp.repeat(jnp.exp(steps), dims[position] // parts).reshape((-1,) + (1,) * (len(dims) - position - 1))

    level = one(*cuts[0])
    for cut in cuts[1:]:
        level = level * one(*cut)
    return level


def centred(rng, shape, width, limit, cuts=(), held_as=jnp.bfloat16):
    values = width * jax.random.normal(rng, shape, jnp.float32)
    if cuts:
        values = values * shard_levels(rng, shape, cuts, -0.22, 0.18)
    return jnp.clip(values, -limit, limit).astype(held_as)


def setup_inputs(seed: int = 0) -> dict:
    splits = jax.random.split(jax.random.key(seed), 6)
    return {
        "queries": draw_queries(jax.random.fold_in(splits[5], 71), 0),
        "keys": draw_keys(jax.random.fold_in(splits[5], 71), 0),
        "values": centred(splits[2], (CLIPS, F, S, D), 1.0, 6.0, ((0, 16), (1, 32))),
        "grad_out": centred(splits[3], (CLIPS, F, S, D), 1.0, 6.0, ((0, 16), (1, 32))),
        "w_out": centred(splits[4], (D, D), D ** -0.5, 0.1875, ((0, 32),)),
    }


def rounded(x):
    return lax.optimization_barrier(x.astype(jnp.bfloat16)).astype(jnp.float32)


def one_clip(args):
    queries, keys, values, grad_out, w_out = args
    scale = 1.0 / (HEAD_DIM ** 0.5)
    shape = (F, S, HEADS, HEAD_DIM)
    qh = queries.astype(jnp.float32).reshape(shape)
    kh = keys.astype(jnp.float32).reshape(shape)
    vh = values.astype(jnp.float32).reshape(shape)
    scores = jnp.einsum('fshd,gshd->shfg', qh, kh) * scale
    prob = jax.nn.softmax(scores, axis=-1)
    prob_b = rounded(prob)
    attn = jnp.einsum('shfg,gshd->fshd', prob_b, vh).astype(jnp.bfloat16)
    dy_rows = grad_out.reshape(F * S, D)
    grad_attn = jnp.dot(dy_rows, w_out.T, preferred_element_type=jnp.float32).astype(jnp.bfloat16)
    ga = grad_attn.astype(jnp.float32).reshape(shape)
    grad_values = jnp.einsum('shfg,fshd->gshd', prob_b, ga).astype(jnp.bfloat16)
    grad_prob = jnp.einsum('fshd,gshd->shfg', ga, vh)
    grad_scores = prob * (grad_prob - jnp.sum(prob * grad_prob, axis=-1, keepdims=True))
    gs_b = rounded(grad_scores)
    grad_queries = (jnp.einsum('shfg,gshd->fshd', gs_b, kh) * scale).astype(jnp.bfloat16)
    grad_keys = (jnp.einsum('shfg,fshd->gshd', gs_b, qh) * scale).astype(jnp.bfloat16)
    attn_rows = attn.reshape(F * S, D)
    weight_sum = jnp.dot(attn_rows.T, dy_rows, preferred_element_type=jnp.float32)
    return (grad_queries.reshape(F, S, D), grad_keys.reshape(F, S, D),
            grad_values.reshape(F, S, D), weight_sum)


def reference(queries, keys, values, grad_out, w_out):
    def mapped(items):
        return one_clip((items[0], items[1], items[2], items[3], w_out))
    gq, gk, gv, sums = lax.map(mapped, (queries, keys, values, grad_out))
    return gq, gk, gv, jnp.sum(sums, axis=0)
```

```python
import jax
import jax.numpy as jnp
from jax import lax
from jax.experimental import pallas as pl
from jax.experimental.pallas import tpu as pltpu
from jax.sharding import PartitionSpec as P

HEADS = 16
HEAD_DIM = 72
WIDTH = 1152
FRAMES = 32
SLOTS = 8
TOKENS = FRAMES * SLOTS
ROWS = 36
QUARTER = ROWS // 4
HALF = 640
SCALE = 1.0 / HEAD_DIM**0.5
LANES = 128
PIECES = ((0, 1, 2), (3, 4), (5, 6), (7, 8))
VMEM = 56 * 1024 * 1024
NN = (((1,), (0,)), ((), ()))
NT = (((1,), (1,)), ((), ()))
TN = (((0,), (0,)), ((), ()))


def mm(a, b, dims):
    return lax.dot_general(a, b, dims, preferred_element_type=jnp.float32)


def window(head):
    first, last = head * HEAD_DIM, (head + 1) * HEAD_DIM - 1
    return first // LANES, last // LANES + 1


def head_mask(head):
    lo, hi = window(head)
    lane = lax.broadcasted_iota(jnp.int32, (1, (hi - lo) * LANES), 1) + lo * LANES
    own = (lane >= head * HEAD_DIM) & (lane < (head + 1) * HEAD_DIM)
    return jnp.where(own, 1.0, 0.0).astype(jnp.bfloat16)


def same_position():
    row = lax.broadcasted_iota(jnp.int32, (TOKENS, TOKENS), 0)
    col = lax.broadcasted_iota(jnp.int32, (TOKENS, TOKENS), 1)
    return jnp.where((row & (SLOTS - 1)) == (col & (SLOTS - 1)), 0.0, -1e30)


def load_tokens(got_ref, which):
    x = got_ref[:, which].astype(jnp.float32).reshape(TOKENS, WIDTH)
    return x.astype(jnp.bfloat16)


class Tiles:
    def __init__(self, store):
        self.open, self.store = {}, store

    def add(self, head, value):
        lo, hi = window(head)
        for tile in range(lo, hi):
            part = value[:, (tile - lo) * LANES : (tile - lo + 1) * LANES]
            self.open[tile] = self.open[tile] + part if tile in self.open else part
        keep = window(head + 1)[0] if head + 1 < HEADS else WIDTH // LANES
        for tile in sorted(self.open):
            if tile < keep:
                self.store(tile, self.open.pop(tile))


def pack_kernel(q_ref, k_ref, v_ref, dy_ref, out_ref, sems):
    copies = [
        pltpu.make_async_copy(ref, out_ref.at[:, i], sems.at[i])
        for i, ref in enumerate((q_ref, k_ref, v_ref, dy_ref))
    ]
    for copy in copies:
        copy.start()
    for copy in copies:
        copy.wait()


def pack(*arrays):
    return pl.pallas_call(
        pack_kernel,
        out_shape=jax.ShapeDtypeStruct((FRAMES, 4, SLOTS, WIDTH), jnp.bfloat16),
        in_specs=[pl.BlockSpec(memory_space=pl.ANY)] * 4,
        out_specs=pl.BlockSpec(memory_space=pltpu.VMEM),
        scratch_shapes=[pltpu.SemaphoreType.DMA((4,))],
        compiler_params=pltpu.CompilerParams(vmem_limit_bytes=VMEM),
        name="pack",
    )(*[a.reshape(FRAMES, SLOTS, WIDTH) for a in arrays])


def forward_kernel(got_ref, order_ref, dy_ref, attn_ref, stats_ref, q_ref, k_ref, v_ref, plain_ref):
    q_ref[...] = load_tokens(got_ref, 0)
    k_ref[...] = load_tokens(got_ref, 1)
    v_ref[...] = load_tokens(got_ref, 2)
    dy_ref[...] = load_tokens(got_ref, 3)
    bias = same_position()

    def store(tile, value):
        plain_ref[:, tile * LANES : (tile + 1) * LANES] = value.astype(jnp.bfloat16)

    attn = Tiles(store)
    lane = lax.broadcasted_iota(jnp.int32, (TOKENS, LANES), 1)
    stats = jnp.zeros((TOKENS, LANES), jnp.float32)
    for head in range(HEADS):
        lo, hi = window(head)
        cols = slice(lo * LANES, hi * LANES)
        mask = head_mask(head)
        scores = mm(q_ref[:, cols], k_ref[:, cols] * mask, NT) * SCALE + bias
        top = jnp.max(scores, axis=1, keepdims=True)
        weight = jnp.exp(scores - top)
        inverse = 1.0 / jnp.sum(weight, axis=1, keepdims=True)
        prob = (weight * inverse).astype(jnp.bfloat16)
        attn.add(head, mm(prob, v_ref[:, cols] * mask, NN))
        stats = jnp.where(lane == head, top, stats)
        stats = jnp.where(lane == HEADS + head, inverse, stats)
    stats_ref[...] = stats.T
    for core in range(2):
        cols = slice(core * HALF, (core + 1) * HALF)
        attn_ref[core] = mm(plain_ref[...], order_ref[:, cols], NN).astype(jnp.bfloat16)


def selection():
    row = lax.broadcasted_iota(jnp.int32, (WIDTH, 2 * HALF), 0)
    col = lax.broadcasted_iota(jnp.int32, (WIDTH, 2 * HALF), 1)
    block, within = row // ROWS, row % ROWS
    place = (block % 2) * HALF + (within // QUARTER) * 144 + (block // 2) * QUARTER + within % QUARTER
    return (place == col).astype(jnp.bfloat16)


def forward(got, order):
    tokens = pltpu.VMEM((TOKENS, WIDTH), jnp.bfloat16)
    return pl.pallas_call(
        forward_kernel,
        out_shape=(
            jax.ShapeDtypeStruct((TOKENS, WIDTH), jnp.bfloat16),
            jax.ShapeDtypeStruct((2, TOKENS, HALF), jnp.bfloat16),
            jax.ShapeDtypeStruct((LANES, TOKENS), jnp.float32),
        ),
        in_specs=[pl.BlockSpec(memory_space=pltpu.VMEM)] * 2,
        out_specs=[pl.BlockSpec(memory_space=pltpu.VMEM)] * 3,
        scratch_shapes=[tokens] * 4,
        compiler_params=pltpu.CompilerParams(vmem_limit_bytes=VMEM),
        name="attention",
    )(got, order)


def backward_kernel(got_ref, dy_ref, stats_ref, w_ref, out_ref, q_ref, k_ref, v_ref, ga_ref, rows_ref):
    q_ref[...] = load_tokens(got_ref, 0)
    k_ref[...] = load_tokens(got_ref, 1)
    v_ref[...] = load_tokens(got_ref, 2)
    for block in range(FRAMES):
        rows_ref[block * ROWS : (block + 1) * ROWS, :] = w_ref[block]
    for tile in range(WIDTH // LANES):
        cols = slice(tile * LANES, (tile + 1) * LANES)
        ga_ref[:, cols] = mm(dy_ref[...], rows_ref[cols, :], NT).astype(jnp.bfloat16)
    bias = same_position()

    def storer(which, scale):
        def store(tile, value):
            if scale is not None:
                value = value * scale
            out_ref[:, which, :, tile * LANES : (tile + 1) * LANES] = value.reshape(
                FRAMES, SLOTS, LANES
            ).astype(jnp.bfloat16)

        return store

    grad_q, grad_k = Tiles(storer(0, SCALE)), Tiles(storer(1, SCALE))
    grad_v = Tiles(storer(2, None))
    for head in range(HEADS):
        lo, hi = window(head)
        cols = slice(lo * LANES, hi * LANES)
        mask = head_mask(head)
        q, k, v, ga = q_ref[:, cols], k_ref[:, cols], v_ref[:, cols], ga_ref[:, cols]
        k_own, ga_own = k * mask, ga * mask
        scores = mm(k_own, q, NT) * SCALE + bias
        top = stats_ref[head : head + 1, :]
        inverse = stats_ref[HEADS + head : HEADS + head + 1, :]
        prob = jnp.exp(scores - top) * inverse
        grad_v.add(head, mm(prob.astype(jnp.bfloat16), ga_own, NN))
        product = prob * mm(v, ga_own, NT)
        total = jnp.sum(product, axis=0, keepdims=True)
        grad_scores = (product - prob * total).astype(jnp.bfloat16)
        grad_k.add(head, mm(grad_scores, q * mask, NN))
        grad_q.add(head, mm(grad_scores, k_own, TN))


def backward(got, dy, stats, weight):
    tokens = pltpu.VMEM((TOKENS, WIDTH), jnp.bfloat16)
    return pl.pallas_call(
        backward_kernel,
        out_shape=jax.ShapeDtypeStruct((FRAMES, 3, SLOTS, WIDTH), jnp.bfloat16),
        in_specs=[pl.BlockSpec(memory_space=pltpu.VMEM)] * 4,
        out_specs=pl.BlockSpec(memory_space=pltpu.VMEM),
        scratch_shapes=[tokens] * 4 + [pltpu.VMEM((WIDTH, WIDTH), jnp.bfloat16)],
        compiler_params=pltpu.CompilerParams(vmem_limit_bytes=VMEM),
        name="attention_gradients",
    )(got, dy, stats, weight)


def weight_kernel(place_ref, attn_ref, attn_in_ref, dy_ref, dy_in_ref, out_ref):
    own = attn_ref[place_ref[0]]
    for tile in range(WIDTH // LANES):
        cols = slice(tile * LANES, (tile + 1) * LANES)
        total = mm(own, dy_ref[:, cols], TN) + mm(attn_in_ref[...], dy_in_ref[:, cols], TN)
        for x in range(4):
            slot = (x - place_ref[1]) & 3
            out_ref[slot, :, cols] = total[x * 144 : (x + 1) * 144].astype(jnp.bfloat16)


def weight_term(place, attn, attn_in, dy, dy_in):
    return pl.pallas_call(
        weight_kernel,
        out_shape=jax.ShapeDtypeStruct((4, 144, WIDTH), jnp.bfloat16),
        in_specs=[pl.BlockSpec(memory_space=pltpu.SMEM)]
        + [pl.BlockSpec(memory_space=pltpu.VMEM)] * 4,
        out_specs=pl.BlockSpec(memory_space=pltpu.VMEM),
        compiler_params=pltpu.CompilerParams(vmem_limit_bytes=VMEM),
        name="weight_term",
    )(place, attn, attn_in, dy, dy_in)


def add_x_kernel(place_ref, a_ref, b_ref, c_ref, d_ref, out_ref):
    for piece, tiles in enumerate(PIECES):
        slot = (piece - place_ref[2]) & 3
        for i in range(3):
            if i < len(tiles):
                cols = slice(tiles[i] * LANES, (tiles[i] + 1) * LANES)
                parts = [r[:, cols].astype(jnp.float32) for r in (a_ref, b_ref, c_ref, d_ref)]
                total = (parts[0] + parts[1]) + (parts[2] + parts[3])
            else:
                total = jnp.zeros((144, LANES), jnp.float32)
            out_ref[slot, :, i * LANES : (i + 1) * LANES] = total.astype(jnp.bfloat16)


def add_x(place, parts):
    return pl.pallas_call(
        add_x_kernel,
        out_shape=jax.ShapeDtypeStruct((4, 144, 3 * LANES), jnp.bfloat16),
        in_specs=[pl.BlockSpec(memory_space=pltpu.SMEM)]
        + [pl.BlockSpec(memory_space=pltpu.VMEM)] * 4,
        out_specs=pl.BlockSpec(memory_space=pltpu.VMEM),
        name="add_x",
    )(place, *parts)


def add_z_kernel(a_ref, b_ref, c_ref, d_ref, out_ref):
    for i in range(3):
        cols = slice(i * LANES, (i + 1) * LANES)
        parts = [r[:, cols].astype(jnp.float32) for r in (a_ref, b_ref, c_ref, d_ref)]
        total = (parts[0] + parts[1]) + (parts[2] + parts[3])
        for block in range(16):
            out_ref[block, i * QUARTER : (i + 1) * QUARTER, :] = total[
                block * QUARTER : (block + 1) * QUARTER
            ]
    out_ref[:, 3 * QUARTER :, :] = jnp.zeros((16, 5, LANES), jnp.float32)


def add_z(parts):
    return pl.pallas_call(
        add_z_kernel,
        out_shape=jax.ShapeDtypeStruct((16, 32, LANES), jnp.float32),
        in_specs=[pl.BlockSpec(memory_space=pltpu.VMEM)] * 4,
        out_specs=pl.BlockSpec(memory_space=pltpu.VMEM),
        name="add_z",
    )(*parts)


def add_frames_kernel(got_ref, out_ref):
    total = jnp.sum(got_ref[...], axis=0)
    for i in range(16):
        out_ref[i] = total


def add_frames(got):
    return pl.pallas_call(
        add_frames_kernel,
        out_shape=jax.ShapeDtypeStruct((16, 32, LANES), jnp.float32),
        in_specs=[pl.BlockSpec(memory_space=pltpu.VMEM)],
        out_specs=pl.BlockSpec(memory_space=pltpu.VMEM),
        name="add_frames",
    )(got)


def assemble_kernel(got_ref, out_ref):
    for piece, tiles in enumerate(PIECES):
        for x in range(4):
            for i, tile in enumerate(tiles):
                out_ref[x * QUARTER : (x + 1) * QUARTER, tile * LANES : (tile + 1) * LANES] = got_ref[
                    piece * 4 + x, i * QUARTER : (i + 1) * QUARTER, :
                ]


def assemble(got):
    return pl.pallas_call(
        assemble_kernel,
        out_shape=jax.ShapeDtypeStruct((ROWS, WIDTH), jnp.float32),
        in_specs=[pl.BlockSpec(memory_space=pltpu.VMEM)],
        out_specs=pl.BlockSpec(memory_space=pltpu.VMEM),
        name="assemble",
    )(got)


def at(y, z, core):
    return y * 4 + z * 2 + core


SWAP_CORE = [(i, i ^ 1) for i in range(FRAMES)]
SAME_CORE = [[at(y, z, c) for y in range(8) for z in range(2)] for c in range(2)]


def all_to_all(x, axis, groups=None):
    return lax.all_to_all(
        x, axis, split_axis=0, concat_axis=0, tiled=True, axis_index_groups=groups
    )


def along_x(x, step):
    return lax.ppermute(
        x, "clip", [(z * 4 + i, z * 4 + (i + step) % 4) for z in range(4) for i in range(4)]
    )


def along_z(x, step):
    return lax.ppermute(
        x, "clip", [(z * 4 + i, (z + step) % 4 * 4 + i) for z in range(4) for i in range(4)]
    )


def on_device(queries, keys, values, grad_out, w_out):
    weight = lax.all_gather(w_out, "frame", axis=0)
    got = all_to_all(pack(queries, keys, values, grad_out), "frame")
    dy, attn, stats = forward(got, selection())

    core = lax.axis_index("frame") & 1
    clip = lax.axis_index("clip")
    place = jnp.stack([core, clip & 3, clip >> 2])
    attn_in = lax.ppermute(lax.dynamic_index_in_dim(attn, 1 - core, 0, False), "frame", SWAP_CORE)
    dy_in = lax.ppermute(dy, "frame", SWAP_CORE)
    term = weight_term(place, attn, attn_in, dy, dy_in)
    term = add_x(place, [term[0]] + [along_x(term[i], i) for i in (1, 2, 3)])
    term = add_z([term[0]] + [along_z(term[i], i) for i in (1, 2, 3)])

    out = all_to_all(backward(got, dy, stats, weight), "frame")

    out, term = lax.optimization_barrier((out, term))
    term = add_frames(all_to_all(term, "frame", SAME_CORE))
    grad_weight = assemble(all_to_all(term, "clip"))
    shape = (1, 1, TOKENS, WIDTH)
    return (
        out[:, 0].reshape(shape),
        out[:, 1].reshape(shape),
        out[:, 2].reshape(shape),
        grad_weight,
    )


def solution(mesh):
    spread = P("clip", "frame", None, None)
    return jax.shard_map(
        on_device,
        mesh=mesh,
        in_specs=(spread, spread, spread, spread, P("frame", None)),
        out_specs=(spread, spread, spread, P("frame", None)),
        check_vma=False,
    )
```

```python
import jax
import jax.numpy as jnp
from jax import lax
from jax.experimental import pallas as pl
from jax.experimental.pallas import tpu as pltpu
from jax.sharding import PartitionSpec as P

HEADS = 16
HEAD_DIM = 72
WIDTH = 1152
FRAMES = 32
SLOTS = 8
TOKENS = FRAMES * SLOTS
ROWS = 36
QUARTER = ROWS // 4
HALF = 640
SCALE = 1.0 / HEAD_DIM**0.5
LANES = 128
TALL = 96
MIB = 1024 * 1024
NN = (((1,), (0,)), ((), ()))
NT = (((1,), (1,)), ((), ()))
TN = (((0,), (0,)), ((), ()))


def mm(a, b, dims):
    return lax.dot_general(a, b, dims, preferred_element_type=jnp.float32)


def window(head):
    first, last = head * HEAD_DIM, (head + 1) * HEAD_DIM - 1
    return first // LANES, last // LANES + 1


def head_mask(head):
    lo, hi = window(head)
    lane = lax.broadcasted_iota(jnp.int32, (1, (hi - lo) * LANES), 1) + lo * LANES
    own = (lane >= head * HEAD_DIM) & (lane < (head + 1) * HEAD_DIM)
    return jnp.where(own, 1.0, 0.0).astype(jnp.bfloat16)


def same_position():
    row = lax.broadcasted_iota(jnp.int32, (TOKENS, TOKENS), 0)
    col = lax.broadcasted_iota(jnp.int32, (TOKENS, TOKENS), 1)
    return jnp.where((row & (SLOTS - 1)) == (col & (SLOTS - 1)), 0.0, -1e30)


def as_tokens(x):
    return x.astype(jnp.float32).reshape(TOKENS, WIDTH).astype(jnp.bfloat16)


class Tiles:
    def __init__(self, store):
        self.open, self.store = {}, store

    def add(self, head, value):
        lo, hi = window(head)
        for tile in range(lo, hi):
            part = value[:, (tile - lo) * LANES : (tile - lo + 1) * LANES]
            self.open[tile] = self.open[tile] + part if tile in self.open else part
        keep = window(head + 1)[0] if head + 1 < HEADS else WIDTH // LANES
        for tile in sorted(self.open):
            if tile < keep:
                self.store(tile, self.open.pop(tile))


def pack_kernel(q_ref, k_ref, v_ref, dy_ref, out_ref, sems):
    copies = [
        pltpu.make_async_copy(ref, out_ref.at[:, i], sems.at[i])
        for i, ref in enumerate((q_ref, k_ref, v_ref, dy_ref))
    ]
    for copy in copies:
        copy.start()
    for copy in copies:
        copy.wait()


def pack(*arrays):
    return pl.pallas_call(
        pack_kernel,
        out_shape=jax.ShapeDtypeStruct((FRAMES, 4, SLOTS, WIDTH), jnp.bfloat16),
        in_specs=[pl.BlockSpec(memory_space=pl.ANY)] * 4,
        out_specs=pl.BlockSpec(memory_space=pltpu.VMEM),
        scratch_shapes=[pltpu.SemaphoreType.DMA((4,))],
        compiler_params=pltpu.CompilerParams(vmem_limit_bytes=60 * MIB),
        name="pack",
    )(*[a.reshape(FRAMES, SLOTS, WIDTH) for a in arrays])


def forward_kernel(
    place_ref, got_ref, order_ref, dy_out, own_out, other_out, stats_ref,
    raw_ref, pick_ref, q_ref, k_ref, v_ref, dy_ref, attn_ref, plain_ref, in_sems, out_sems,
):
    arrive = [pltpu.make_async_copy(got_ref.at[:, i], raw_ref.at[i], in_sems.at[i]) for i in range(4)]
    arrive.append(pltpu.make_async_copy(order_ref, pick_ref, in_sems.at[4]))
    for copy in arrive:
        copy.start()
    for i, ref in enumerate((q_ref, k_ref, v_ref, dy_ref)):
        arrive[i].wait()
        ref[...] = as_tokens(raw_ref[i])
    leave = [pltpu.make_async_copy(dy_ref, dy_out, out_sems.at[0])]
    leave[0].start()
    bias = same_position()

    def store(tile, value):
        plain_ref[:, tile * LANES : (tile + 1) * LANES] = value.astype(jnp.bfloat16)

    attn = Tiles(store)
    for head in range(HEADS):
        lo, hi = window(head)
        cols = slice(lo * LANES, hi * LANES)
        mask = head_mask(head)
        scores = mm(k_ref[:, cols] * mask, q_ref[:, cols], NT) * SCALE + bias
        top = jnp.max(scores, axis=0, keepdims=True)
        weight = jnp.exp(scores - top)
        inverse = 1.0 / jnp.sum(weight, axis=0, keepdims=True)
        stats_ref[head : head + 1, :] = top
        stats_ref[HEADS + head : HEADS + head + 1, :] = inverse
        attn.add(head, mm((weight * inverse).astype(jnp.bfloat16), v_ref[:, cols] * mask, TN))
    arrive[4].wait()
    for core in range(2):
        cols = slice(core * HALF, (core + 1) * HALF)
        attn_ref[core] = mm(plain_ref[...], pick_ref[:, cols], NN).astype(jnp.bfloat16)
    core = place_ref[0]
    leave.append(pltpu.make_async_copy(attn_ref.at[core], own_out, out_sems.at[1]))
    leave.append(pltpu.make_async_copy(attn_ref.at[1 - core], other_out, out_sems.at[2]))
    for copy in leave[1:]:
        copy.start()
    for copy in leave:
        copy.wait()


def selection():
    row = lax.broadcasted_iota(jnp.int32, (WIDTH, 2 * HALF), 0)
    col = lax.broadcasted_iota(jnp.int32, (WIDTH, 2 * HALF), 1)
    block, within = row // ROWS, row % ROWS
    place = (block % 2) * HALF + (within // QUARTER) * 144 + (block // 2) * QUARTER + within % QUARTER
    return (place == col).astype(jnp.bfloat16)


def forward(place, got, order):
    tokens = (TOKENS, WIDTH)
    halves = (2, TOKENS, HALF)
    return pl.pallas_call(
        forward_kernel,
        out_shape=(
            jax.ShapeDtypeStruct(tokens, jnp.bfloat16),
            jax.ShapeDtypeStruct((TOKENS, HALF), jnp.bfloat16),
            jax.ShapeDtypeStruct((TOKENS, HALF), jnp.bfloat16),
            jax.ShapeDtypeStruct((2 * HEADS, TOKENS), jnp.float32),
        ),
        in_specs=[pl.BlockSpec(memory_space=pltpu.SMEM)]
        + [pl.BlockSpec(memory_space=pl.ANY)] * 2,
        out_specs=[pl.BlockSpec(memory_space=pltpu.HBM)] * 3 + [pl.BlockSpec(memory_space=pltpu.VMEM)],
        scratch_shapes=[
            pltpu.VMEM((4, FRAMES, SLOTS, WIDTH), jnp.bfloat16),
            pltpu.VMEM((WIDTH, 2 * HALF), jnp.bfloat16),
            *[pltpu.VMEM(tokens, jnp.bfloat16)] * 4,
            pltpu.VMEM(halves, jnp.bfloat16),
            pltpu.VMEM(tokens, jnp.bfloat16),
            pltpu.SemaphoreType.DMA((5,)),
            pltpu.SemaphoreType.DMA((3,)),
        ],
        compiler_params=pltpu.CompilerParams(vmem_limit_bytes=48 * MIB),
        name="attention",
    )(place, got, order)


def backward_kernel(
    got_ref, dy_in, stats_ref, w_in, after_ref, out_hbm,
    raw_ref, q_ref, k_ref, v_ref, dy_ref, w_ref, ga_ref, across_ref, rows_ref, prob_ref, out_ref,
    sems, out_sems,
):
    arrive = [
        pltpu.make_async_copy(got_ref.at[:, i], raw_ref.at[i], sems.at[i]) for i in range(3)
    ]
    arrive.append(pltpu.make_async_copy(dy_in, dy_ref, sems.at[3]))
    for i in range(4):
        part = pl.ds(8 * i, 8)
        arrive.append(pltpu.make_async_copy(w_in.at[part], w_ref.at[part], sems.at[4 + i]))
    for i in (0, 1, 4, 5, 6, 7, 3, 2):
        arrive[i].start()
    bias = same_position()
    for i, ref in enumerate((q_ref, k_ref)):
        arrive[i].wait()
        ref[...] = as_tokens(raw_ref[i])
    for head in range(HEADS):
        lo, hi = window(head)
        cols = slice(lo * LANES, hi * LANES)
        scores = mm(k_ref[:, cols] * head_mask(head), q_ref[:, cols], NT) * SCALE + bias
        top = stats_ref[head : head + 1, :]
        inverse = stats_ref[HEADS + head : HEADS + head + 1, :]
        prob_ref[head] = jnp.exp(scores - top) * inverse
    for i in range(4):
        arrive[4 + i].wait()
        for block in range(8 * i, 8 * i + 8):
            rows_ref[block * ROWS : (block + 1) * ROWS, :] = w_ref[block]
    arrive[3].wait()
    for tile in range(WIDTH // LANES):
        cols = slice(tile * LANES, (tile + 1) * LANES)
        ga = mm(dy_ref[...], rows_ref[cols, :], NT)
        ga_ref[:, cols] = ga.astype(jnp.bfloat16)
        across_ref[cols, :] = ga.T.astype(jnp.bfloat16)
    arrive[2].wait()
    v_ref[...] = as_tokens(raw_ref[2])

    leave = []

    def storer(which, scale):
        def store(tile, value):
            if scale is not None:
                value = value * scale
            out_ref[:, which, :, tile * LANES : (tile + 1) * LANES] = value.reshape(
                FRAMES, SLOTS, LANES
            ).astype(jnp.bfloat16)
            if tile % 3 == 2:
                part = (slice(None), which, slice(None), pl.ds((tile - 2) * LANES, 3 * LANES))
                sem = out_sems.at[3 * which + tile // 3]
                leave.append(pltpu.make_async_copy(out_ref.at[part], out_hbm.at[part], sem))
                leave[-1].start()

        return store

    grad_q, grad_k = Tiles(storer(0, SCALE)), Tiles(storer(1, SCALE))
    grad_v = Tiles(storer(2, None))
    for head in range(HEADS):
        lo, hi = window(head)
        cols = slice(lo * LANES, hi * LANES)
        mask = head_mask(head)
        prob = prob_ref[head]
        grad_v.add(head, mm(prob.astype(jnp.bfloat16), ga_ref[:, cols] * mask, NN))
        product = prob * mm(v_ref[:, cols] * mask, across_ref[cols, :], NN)
        total = jnp.sum(product, axis=0, keepdims=True)
        grad_scores = (product - prob * total).astype(jnp.bfloat16)
        grad_k.add(head, mm(grad_scores, q_ref[:, cols] * mask, NN))
        grad_q.add(head, mm(grad_scores, k_ref[:, cols] * mask, TN))
    for copy in leave:
        copy.wait()


def backward(got, dy, stats, weight, after):
    tokens = pltpu.VMEM((TOKENS, WIDTH), jnp.bfloat16)
    return pl.pallas_call(
        backward_kernel,
        out_shape=pltpu.HBM((FRAMES, 3, SLOTS, WIDTH), jnp.bfloat16),
        in_specs=[
            pl.BlockSpec(memory_space=pl.ANY),
            pl.BlockSpec(memory_space=pl.ANY),
            pl.BlockSpec(memory_space=pltpu.VMEM),
            pl.BlockSpec(memory_space=pl.ANY),
            pl.BlockSpec(memory_space=pl.ANY),
        ],
        out_specs=pl.BlockSpec(memory_space=pltpu.HBM),
        scratch_shapes=[
            pltpu.VMEM((3, FRAMES, SLOTS, WIDTH), jnp.bfloat16),
            *[tokens] * 4,
            pltpu.VMEM((FRAMES, ROWS, WIDTH), jnp.bfloat16),
            tokens,
            pltpu.VMEM((WIDTH, TOKENS), jnp.bfloat16),
            pltpu.VMEM((WIDTH, WIDTH), jnp.bfloat16),
            pltpu.VMEM((HEADS, TOKENS, TOKENS), jnp.float32),
            pltpu.VMEM((FRAMES, 3, SLOTS, WIDTH), jnp.bfloat16),
            pltpu.SemaphoreType.DMA((8,)),
            pltpu.SemaphoreType.DMA((9,)),
        ],
        compiler_params=pltpu.CompilerParams(vmem_limit_bytes=52 * MIB),
        name="attention_gradients",
    )(got, dy, stats, weight, after)


def weight_kernel(
    attn_in, other_in, dy_in, dy_other_in, out_hbm, token_ref,
    attn_ref, other_ref, dy_ref, dy_other_ref, out_ref, sems, out_sems,
):
    pairs = (
        (attn_in, attn_ref),
        (dy_in, dy_ref),
        (other_in, other_ref),
        (dy_other_in, dy_other_ref),
    )
    arrive = [pltpu.make_async_copy(src, dst, sems.at[i]) for i, (src, dst) in enumerate(pairs)]
    for copy in arrive:
        copy.start()
    for copy in arrive:
        copy.wait()
    leave = []
    for tile in range(WIDTH // LANES):
        cols = slice(tile * LANES, (tile + 1) * LANES)
        total = mm(attn_ref[...], dy_ref[:, cols], TN)
        total += mm(other_ref[...], dy_other_ref[:, cols], TN)
        for x in range(4):
            out_ref[x, :, cols] = total[x * 144 : (x + 1) * 144].astype(jnp.bfloat16)
        if tile % 3 == 2:
            part = (slice(None), slice(None), pl.ds((tile - 2) * LANES, 3 * LANES))
            leave.append(
                pltpu.make_async_copy(out_ref.at[part], out_hbm.at[part], out_sems.at[tile // 3])
            )
            leave[-1].start()
    for copy in leave:
        copy.wait()
    token_ref[...] = jnp.zeros_like(token_ref)


def weight_term(attn, attn_in, dy, dy_in):
    half = pltpu.VMEM((TOKENS, HALF), jnp.bfloat16)
    tokens = pltpu.VMEM((TOKENS, WIDTH), jnp.bfloat16)
    return pl.pallas_call(
        weight_kernel,
        out_shape=(
            pltpu.HBM((4, 144, WIDTH), jnp.bfloat16),
            jax.ShapeDtypeStruct((8, LANES), jnp.float32),
        ),
        in_specs=[pl.BlockSpec(memory_space=pl.ANY)] * 4,
        out_specs=[pl.BlockSpec(memory_space=pltpu.HBM), pl.BlockSpec(memory_space=pltpu.VMEM)],
        scratch_shapes=[
            half,
            half,
            tokens,
            tokens,
            pltpu.VMEM((4, 144, WIDTH), jnp.bfloat16),
            pltpu.SemaphoreType.DMA((4,)),
            pltpu.SemaphoreType.DMA((3,)),
        ],
        compiler_params=pltpu.CompilerParams(vmem_limit_bytes=12 * MIB),
        name="weight_term",
    )(attn, attn_in, dy, dy_in)


def add_x_kernel(got_ref, out_ref):
    for tile in range(WIDTH // LANES):
        cols = slice(tile * LANES, (tile + 1) * LANES)
        parts = [got_ref[x, :, cols].astype(jnp.float32) for x in range(4)]
        total = (parts[0] + parts[1]) + (parts[2] + parts[3])
        out_ref[:, cols] = total.astype(jnp.bfloat16)


def add_x(got):
    return pl.pallas_call(
        add_x_kernel,
        out_shape=jax.ShapeDtypeStruct((144, WIDTH), jnp.bfloat16),
        in_specs=[pl.BlockSpec(memory_space=pltpu.VMEM)],
        out_specs=pl.BlockSpec(memory_space=pltpu.VMEM),
        compiler_params=pltpu.CompilerParams(vmem_limit_bytes=6 * MIB),
        name="add_x",
    )(got)


def add_z_kernel(a_ref, b_ref, out_ref, sum_ref):
    sum_ref[:, 9 * QUARTER :, :] = jnp.zeros((16, TALL - 9 * QUARTER, LANES), jnp.float32)
    for tile in range(WIDTH // LANES):
        cols = slice(tile * LANES, (tile + 1) * LANES)
        total = a_ref[:, cols].astype(jnp.float32) + b_ref[:, cols].astype(jnp.float32)
        for block in range(16):
            sum_ref[block, tile * QUARTER : (tile + 1) * QUARTER, :] = total[
                block * QUARTER : (block + 1) * QUARTER
            ]
    out_ref[...] = sum_ref[...].astype(jnp.bfloat16)


def add_z(a, b):
    return pl.pallas_call(
        add_z_kernel,
        out_shape=jax.ShapeDtypeStruct((16, TALL, LANES), jnp.bfloat16),
        in_specs=[pl.BlockSpec(memory_space=pltpu.VMEM)] * 2,
        out_specs=pl.BlockSpec(memory_space=pltpu.VMEM),
        scratch_shapes=[pltpu.VMEM((16, TALL, LANES), jnp.float32)],
        compiler_params=pltpu.CompilerParams(vmem_limit_bytes=6 * MIB),
        name="add_z",
    )(a, b)


def add_frames_kernel(got_ref, out_ref):
    total = got_ref[0].astype(jnp.float32)
    for i in range(1, 16):
        total += got_ref[i].astype(jnp.float32)
    for i in range(4):
        out_ref[i] = total


def add_frames(got):
    return pl.pallas_call(
        add_frames_kernel,
        out_shape=jax.ShapeDtypeStruct((4, TALL, LANES), jnp.float32),
        in_specs=[pl.BlockSpec(memory_space=pltpu.VMEM)],
        out_specs=pl.BlockSpec(memory_space=pltpu.VMEM),
        compiler_params=pltpu.CompilerParams(vmem_limit_bytes=4 * MIB),
        name="add_frames",
    )(got)


def assemble_kernel(got_ref, out_ref):
    for x in range(4):
        for tile in range(WIDTH // LANES):
            out_ref[x * QUARTER : (x + 1) * QUARTER, tile * LANES : (tile + 1) * LANES] = got_ref[
                x, tile * QUARTER : (tile + 1) * QUARTER, :
            ]


def assemble(got):
    return pl.pallas_call(
        assemble_kernel,
        out_shape=jax.ShapeDtypeStruct((ROWS, WIDTH), jnp.float32),
        in_specs=[pl.BlockSpec(memory_space=pltpu.VMEM)],
        out_specs=pl.BlockSpec(memory_space=pltpu.VMEM),
        compiler_params=pltpu.CompilerParams(vmem_limit_bytes=4 * MIB),
        name="assemble",
    )(got)


def at(y, z, core):
    return y * 4 + z * 2 + core


SWAP_CORE = [(i, i ^ 1) for i in range(FRAMES)]
SAME_CORE = [[at(y, z, c) for y in range(8) for z in range(2)] for c in range(2)]
ALONG_X = [[z * 4 + x for x in range(4)] for z in range(4)]


def all_to_all(x, axis, groups=None):
    return lax.all_to_all(
        x, axis, split_axis=0, concat_axis=0, tiled=True, axis_index_groups=groups
    )


def swap_z(x, bits):
    return lax.ppermute(x, "clip", [(z * 4 + i, (z ^ bits) * 4 + i) for z in range(4) for i in range(4)])


def on_device(queries, keys, values, grad_out, w_out):
    weight = lax.all_gather(w_out, "frame", axis=0)
    clip = lax.axis_index("clip")
    place = jnp.stack([lax.axis_index("frame") & 1, clip & 3, clip >> 2])
    got = all_to_all(pack(queries, keys, values, grad_out), "frame")
    dy, attn, other, stats = forward(place, got, selection())

    attn_in = lax.ppermute(other, "frame", SWAP_CORE)
    dy_in = lax.ppermute(dy, "frame", SWAP_CORE)
    term, token = weight_term(attn, attn_in, dy, dy_in)
    out = backward(got, dy, stats, weight, token)
    term = add_x(all_to_all(term, "clip", ALONG_X))
    out = all_to_all(out, "frame")
    pair = term.astype(jnp.float32) + swap_z(term, 1).astype(jnp.float32)
    pair = pair.astype(jnp.bfloat16)
    term = add_z(pair, swap_z(pair, 3))

    out, term = lax.optimization_barrier((out, term))
    term = add_frames(all_to_all(term, "frame", SAME_CORE))
    grad_weight = assemble(all_to_all(term, "clip", ALONG_X))
    shape = (1, 1, TOKENS, WIDTH)
    return (
        out[:, 0].reshape(shape),
        out[:, 1].reshape(shape),
        out[:, 2].reshape(shape),
        grad_weight,
    )


def solution(mesh):
    spread = P("clip", "frame", None, None)
    return jax.shard_map(
        on_device,
        mesh=mesh,
        in_specs=(spread, spread, spread, spread, P("frame", None)),
        out_specs=(spread, spread, spread, P("frame", None)),
        check_vma=False,
    )
```

```python
import jax
import jax.numpy as jnp
from jax import lax
from jax.experimental import pallas as pl
from jax.experimental.pallas import tpu as pltpu
from jax.sharding import PartitionSpec as P

HEADS = 16
HEAD_DIM = 72
WIDTH = 1152
FRAMES = 32
SLOTS = 8
TOKENS = FRAMES * SLOTS
ROWS = 36
QUARTER = ROWS // 4
HALF = 640
SCALE = 1.0 / HEAD_DIM**0.5
LANES = 128
TALL = 96
MIB = 1024 * 1024
NN = (((1,), (0,)), ((), ()))
NT = (((1,), (1,)), ((), ()))
TN = (((0,), (0,)), ((), ()))


def mm(a, b, dims):
    return lax.dot_general(a, b, dims, preferred_element_type=jnp.float32)


def window(head):
    first, last = head * HEAD_DIM, (head + 1) * HEAD_DIM - 1
    return first // LANES, last // LANES + 1


def head_mask(head):
    lo, hi = window(head)
    lane = lax.broadcasted_iota(jnp.int32, (1, (hi - lo) * LANES), 1) + lo * LANES
    own = (lane >= head * HEAD_DIM) & (lane < (head + 1) * HEAD_DIM)
    return jnp.where(own, 1.0, 0.0).astype(jnp.bfloat16)


def same_position():
    row = lax.broadcasted_iota(jnp.int32, (TOKENS, TOKENS), 0)
    col = lax.broadcasted_iota(jnp.int32, (TOKENS, TOKENS), 1)
    return jnp.where((row & (SLOTS - 1)) == (col & (SLOTS - 1)), 0.0, -1e30)


def as_tokens(x):
    return x.astype(jnp.float32).reshape(TOKENS, WIDTH).astype(jnp.bfloat16)


class Tiles:
    def __init__(self, store):
        self.open, self.store = {}, store

    def add(self, head, value):
        lo, hi = window(head)
        for tile in range(lo, hi):
            part = value[:, (tile - lo) * LANES : (tile - lo + 1) * LANES]
            self.open[tile] = self.open[tile] + part if tile in self.open else part
        keep = window(head + 1)[0] if head + 1 < HEADS else WIDTH // LANES
        for tile in sorted(self.open):
            if tile < keep:
                self.store(tile, self.open.pop(tile))


def pack_kernel(q_ref, k_ref, v_ref, dy_ref, out_ref, sems):
    copies = [
        pltpu.make_async_copy(ref, out_ref.at[:, i], sems.at[i])
        for i, ref in enumerate((q_ref, k_ref, v_ref, dy_ref))
    ]
    for copy in copies:
        copy.start()
    for copy in copies:
        copy.wait()


def pack(*arrays):
    return pl.pallas_call(
        pack_kernel,
        out_shape=jax.ShapeDtypeStruct((FRAMES, 4, SLOTS, WIDTH), jnp.bfloat16),
        in_specs=[pl.BlockSpec(memory_space=pl.ANY)] * 4,
        out_specs=pl.BlockSpec(memory_space=pltpu.VMEM),
        scratch_shapes=[pltpu.SemaphoreType.DMA((4,))],
        compiler_params=pltpu.CompilerParams(vmem_limit_bytes=60 * MIB),
        name="pack",
    )(*[a.reshape(FRAMES, SLOTS, WIDTH) for a in arrays])


def forward_kernel(
    place_ref, got_ref, order_ref, dy_out, own_out, send_out, stats_ref,
    pick_ref, q_ref, k_ref, v_ref, dy_ref, attn_ref, plain_ref, in_sem, out_sems,
):
    arrive = pltpu.make_async_copy(order_ref, pick_ref, in_sem)
    arrive.start()
    for i, ref in enumerate((q_ref, k_ref, v_ref, dy_ref)):
        ref[...] = as_tokens(got_ref[:, i])
    leave = [
        pltpu.make_async_copy(dy_ref, dy_out, out_sems.at[0]),
        pltpu.make_async_copy(dy_ref, send_out.at[:, pl.ds(HALF, WIDTH)], out_sems.at[3]),
    ]
    for copy in leave:
        copy.start()
    bias = same_position()

    def store(tile, value):
        plain_ref[:, tile * LANES : (tile + 1) * LANES] = value.astype(jnp.bfloat16)

    attn = Tiles(store)
    for head in range(HEADS):
        lo, hi = window(head)
        cols = slice(lo * LANES, hi * LANES)
        mask = head_mask(head)
        scores = mm(k_ref[:, cols] * mask, q_ref[:, cols], NT) * SCALE + bias
        top = jnp.max(scores, axis=0, keepdims=True)
        weight = jnp.exp(scores - top)
        inverse = 1.0 / jnp.sum(weight, axis=0, keepdims=True)
        stats_ref[head : head + 1, :] = top
        stats_ref[HEADS + head : HEADS + head + 1, :] = inverse
        attn.add(head, mm((weight * inverse).astype(jnp.bfloat16), v_ref[:, cols] * mask, TN))
    arrive.wait()
    for core in range(2):
        cols = slice(core * HALF, (core + 1) * HALF)
        attn_ref[core] = mm(plain_ref[...], pick_ref[:, cols], NN).astype(jnp.bfloat16)
    core = place_ref[0]
    leave.append(pltpu.make_async_copy(attn_ref.at[core], own_out, out_sems.at[1]))
    leave.append(
        pltpu.make_async_copy(attn_ref.at[1 - core], send_out.at[:, pl.ds(0, HALF)], out_sems.at[2])
    )
    for copy in leave[2:]:
        copy.start()
    for copy in leave:
        copy.wait()


def selection():
    row = lax.broadcasted_iota(jnp.int32, (WIDTH, 2 * HALF), 0)
    col = lax.broadcasted_iota(jnp.int32, (WIDTH, 2 * HALF), 1)
    block, within = row // ROWS, row % ROWS
    place = (block % 2) * HALF + (within // QUARTER) * 144 + (block // 2) * QUARTER + within % QUARTER
    return (place == col).astype(jnp.bfloat16)


def forward(place, got, order):
    tokens = (TOKENS, WIDTH)
    halves = (2, TOKENS, HALF)
    return pl.pallas_call(
        forward_kernel,
        out_shape=(
            jax.ShapeDtypeStruct(tokens, jnp.bfloat16),
            jax.ShapeDtypeStruct((TOKENS, HALF), jnp.bfloat16),
            jax.ShapeDtypeStruct((TOKENS, HALF + WIDTH), jnp.bfloat16),
            jax.ShapeDtypeStruct((2 * HEADS, TOKENS), jnp.float32),
        ),
        in_specs=[pl.BlockSpec(memory_space=pltpu.SMEM)]
        + [pl.BlockSpec(memory_space=pltpu.VMEM), pl.BlockSpec(memory_space=pl.ANY)],
        out_specs=[pl.BlockSpec(memory_space=pltpu.HBM)] * 3 + [pl.BlockSpec(memory_space=pltpu.VMEM)],
        scratch_shapes=[
            pltpu.VMEM((WIDTH, 2 * HALF), jnp.bfloat16),
            *[pltpu.VMEM(tokens, jnp.bfloat16)] * 4,
            pltpu.VMEM(halves, jnp.bfloat16),
            pltpu.VMEM(tokens, jnp.bfloat16),
            pltpu.SemaphoreType.DMA,
            pltpu.SemaphoreType.DMA((4,)),
        ],
        compiler_params=pltpu.CompilerParams(vmem_limit_bytes=48 * MIB),
        name="attention",
    )(place, got, order)


def backward_kernel(
    got_ref, dy_in, stats_ref, w_in, after_ref, out_hbm,
    raw_ref, q_ref, k_ref, v_ref, dy_ref, w_ref, ga_ref, across_ref, rows_ref, prob_ref, out_ref,
    sems, out_sems,
):
    arrive = [
        pltpu.make_async_copy(got_ref.at[:, i], raw_ref.at[i], sems.at[i]) for i in range(3)
    ]
    arrive.append(pltpu.make_async_copy(dy_in, dy_ref, sems.at[3]))
    for i in range(4):
        part = pl.ds(8 * i, 8)
        arrive.append(pltpu.make_async_copy(w_in.at[part], w_ref.at[part], sems.at[4 + i]))
    for i in (0, 1, 4, 5, 6, 7, 3, 2):
        arrive[i].start()
    bias = same_position()
    for i, ref in enumerate((q_ref, k_ref)):
        arrive[i].wait()
        ref[...] = as_tokens(raw_ref[i])
    for head in range(HEADS):
        lo, hi = window(head)
        cols = slice(lo * LANES, hi * LANES)
        scores = mm(k_ref[:, cols] * head_mask(head), q_ref[:, cols], NT) * SCALE + bias
        top = stats_ref[head : head + 1, :]
        inverse = stats_ref[HEADS + head : HEADS + head + 1, :]
        prob_ref[head] = jnp.exp(scores - top) * inverse
    for i in range(4):
        arrive[4 + i].wait()
        for block in range(8 * i, 8 * i + 8):
            rows_ref[block * ROWS : (block + 1) * ROWS, :] = w_ref[block]
    arrive[3].wait()
    for tile in range(WIDTH // LANES):
        cols = slice(tile * LANES, (tile + 1) * LANES)
        ga = mm(dy_ref[...], rows_ref[cols, :], NT)
        ga_ref[:, cols] = ga.astype(jnp.bfloat16)
        across_ref[cols, :] = ga.T.astype(jnp.bfloat16)
    arrive[2].wait()
    v_ref[...] = as_tokens(raw_ref[2])

    leave = []

    def storer(which, scale):
        def store(tile, value):
            if scale is not None:
                value = value * scale
            out_ref[:, which, :, tile * LANES : (tile + 1) * LANES] = value.reshape(
                FRAMES, SLOTS, LANES
            ).astype(jnp.bfloat16)
            if tile % 3 == 2:
                part = (slice(None), which, slice(None), pl.ds((tile - 2) * LANES, 3 * LANES))
                sem = out_sems.at[3 * which + tile // 3]
                leave.append(pltpu.make_async_copy(out_ref.at[part], out_hbm.at[part], sem))
                leave[-1].start()

        return store

    grad_q, grad_k = Tiles(storer(0, SCALE)), Tiles(storer(1, SCALE))
    grad_v = Tiles(storer(2, None))
    for head in range(HEADS):
        lo, hi = window(head)
        cols = slice(lo * LANES, hi * LANES)
        mask = head_mask(head)
        prob = prob_ref[head]
        grad_v.add(head, mm(prob.astype(jnp.bfloat16), ga_ref[:, cols] * mask, NN))
        product = prob * mm(v_ref[:, cols] * mask, across_ref[cols, :], NN)
        total = jnp.sum(product, axis=0, keepdims=True)
        grad_scores = (product - prob * total).astype(jnp.bfloat16)
        grad_k.add(head, mm(grad_scores, q_ref[:, cols] * mask, NN))
        grad_q.add(head, mm(grad_scores, k_ref[:, cols] * mask, TN))
    for copy in leave:
        copy.wait()


def backward(got, dy, stats, weight, after):
    tokens = pltpu.VMEM((TOKENS, WIDTH), jnp.bfloat16)
    return pl.pallas_call(
        backward_kernel,
        out_shape=pltpu.HBM((FRAMES, 3, SLOTS, WIDTH), jnp.bfloat16),
        in_specs=[
            pl.BlockSpec(memory_space=pl.ANY),
            pl.BlockSpec(memory_space=pl.ANY),
            pl.BlockSpec(memory_space=pltpu.VMEM),
            pl.BlockSpec(memory_space=pl.ANY),
            pl.BlockSpec(memory_space=pl.ANY),
        ],
        out_specs=pl.BlockSpec(memory_space=pltpu.HBM),
        scratch_shapes=[
            pltpu.VMEM((3, FRAMES, SLOTS, WIDTH), jnp.bfloat16),
            *[tokens] * 4,
            pltpu.VMEM((FRAMES, ROWS, WIDTH), jnp.bfloat16),
            tokens,
            pltpu.VMEM((WIDTH, TOKENS), jnp.bfloat16),
            pltpu.VMEM((WIDTH, WIDTH), jnp.bfloat16),
            pltpu.VMEM((HEADS, TOKENS, TOKENS), jnp.float32),
            pltpu.VMEM((FRAMES, 3, SLOTS, WIDTH), jnp.bfloat16),
            pltpu.SemaphoreType.DMA((8,)),
            pltpu.SemaphoreType.DMA((9,)),
        ],
        compiler_params=pltpu.CompilerParams(vmem_limit_bytes=52 * MIB),
        name="attention_gradients",
    )(got, dy, stats, weight, after)


def weight_kernel(
    attn_in, dy_in, other_in, out_hbm, token_ref,
    attn_ref, other_ref, dy_ref, dy_other_ref, out_ref, sems, out_sems,
):
    pairs = (
        (attn_in, attn_ref),
        (dy_in, dy_ref),
        (other_in.at[:, pl.ds(0, HALF)], other_ref),
        (other_in.at[:, pl.ds(HALF, WIDTH)], dy_other_ref),
    )
    arrive = [pltpu.make_async_copy(src, dst, sems.at[i]) for i, (src, dst) in enumerate(pairs)]
    for copy in arrive:
        copy.start()
    for copy in arrive:
        copy.wait()
    leave = []
    for tile in range(WIDTH // LANES):
        cols = slice(tile * LANES, (tile + 1) * LANES)
        total = mm(attn_ref[...], dy_ref[:, cols], TN)
        total += mm(other_ref[...], dy_other_ref[:, cols], TN)
        for x in range(4):
            out_ref[x, :, cols] = total[x * 144 : (x + 1) * 144].astype(jnp.bfloat16)
        if tile % 3 == 2:
            part = (slice(None), slice(None), pl.ds((tile - 2) * LANES, 3 * LANES))
            leave.append(
                pltpu.make_async_copy(out_ref.at[part], out_hbm.at[part], out_sems.at[tile // 3])
            )
            leave[-1].start()
    for copy in leave:
        copy.wait()
    token_ref[...] = jnp.zeros_like(token_ref)


def weight_term(attn, dy, other):
    half = pltpu.VMEM((TOKENS, HALF), jnp.bfloat16)
    tokens = pltpu.VMEM((TOKENS, WIDTH), jnp.bfloat16)
    return pl.pallas_call(
        weight_kernel,
        out_shape=(
            pltpu.HBM((4, 144, WIDTH), jnp.bfloat16),
            jax.ShapeDtypeStruct((8, LANES), jnp.float32),
        ),
        in_specs=[pl.BlockSpec(memory_space=pl.ANY)] * 3,
        out_specs=[pl.BlockSpec(memory_space=pltpu.HBM), pl.BlockSpec(memory_space=pltpu.VMEM)],
        scratch_shapes=[
            half,
            half,
            tokens,
            tokens,
            pltpu.VMEM((4, 144, WIDTH), jnp.bfloat16),
            pltpu.SemaphoreType.DMA((4,)),
            pltpu.SemaphoreType.DMA((3,)),
        ],
        compiler_params=pltpu.CompilerParams(vmem_limit_bytes=12 * MIB),
        name="weight_term",
    )(attn, dy, other)


def add_x_kernel(got_ref, out_ref):
    for tile in range(WIDTH // LANES):
        cols = slice(tile * LANES, (tile + 1) * LANES)
        parts = [got_ref[x, :, cols].astype(jnp.float32) for x in range(4)]
        total = (parts[0] + parts[1]) + (parts[2] + parts[3])
        out_ref[:, cols] = total.astype(jnp.bfloat16)


def add_x(got):
    return pl.pallas_call(
        add_x_kernel,
        out_shape=jax.ShapeDtypeStruct((144, WIDTH), jnp.bfloat16),
        in_specs=[pl.BlockSpec(memory_space=pltpu.VMEM)],
        out_specs=pl.BlockSpec(memory_space=pltpu.VMEM),
        compiler_params=pltpu.CompilerParams(vmem_limit_bytes=6 * MIB),
        name="add_x",
    )(got)


def add_z_kernel(a_ref, b_ref, out_ref, sum_ref):
    sum_ref[:, 9 * QUARTER :, :] = jnp.zeros((16, TALL - 9 * QUARTER, LANES), jnp.float32)
    for tile in range(WIDTH // LANES):
        cols = slice(tile * LANES, (tile + 1) * LANES)
        total = a_ref[:, cols].astype(jnp.float32) + b_ref[:, cols].astype(jnp.float32)
        for block in range(16):
            sum_ref[block, tile * QUARTER : (tile + 1) * QUARTER, :] = total[
                block * QUARTER : (block + 1) * QUARTER
            ]
    out_ref[...] = sum_ref[...].astype(jnp.bfloat16)


def add_z(a, b):
    return pl.pallas_call(
        add_z_kernel,
        out_shape=jax.ShapeDtypeStruct((16, TALL, LANES), jnp.bfloat16),
        in_specs=[pl.BlockSpec(memory_space=pltpu.VMEM)] * 2,
        out_specs=pl.BlockSpec(memory_space=pltpu.VMEM),
        scratch_shapes=[pltpu.VMEM((16, TALL, LANES), jnp.float32)],
        compiler_params=pltpu.CompilerParams(vmem_limit_bytes=6 * MIB),
        name="add_z",
    )(a, b)


def add_frames_kernel(got_ref, out_ref):
    total = got_ref[0].astype(jnp.float32)
    for i in range(1, 16):
        total += got_ref[i].astype(jnp.float32)
    for i in range(4):
        out_ref[i] = total


def add_frames(got):
    return pl.pallas_call(
        add_frames_kernel,
        out_shape=jax.ShapeDtypeStruct((4, TALL, LANES), jnp.float32),
        in_specs=[pl.BlockSpec(memory_space=pltpu.VMEM)],
        out_specs=pl.BlockSpec(memory_space=pltpu.VMEM),
        compiler_params=pltpu.CompilerParams(vmem_limit_bytes=4 * MIB),
        name="add_frames",
    )(got)


def assemble_kernel(got_ref, out_ref):
    for x in range(4):
        for tile in range(WIDTH // LANES):
            out_ref[x * QUARTER : (x + 1) * QUARTER, tile * LANES : (tile + 1) * LANES] = got_ref[
                x, tile * QUARTER : (tile + 1) * QUARTER, :
            ]


def assemble(got):
    return pl.pallas_call(
        assemble_kernel,
        out_shape=jax.ShapeDtypeStruct((ROWS, WIDTH), jnp.float32),
        in_specs=[pl.BlockSpec(memory_space=pltpu.VMEM)],
        out_specs=pl.BlockSpec(memory_space=pltpu.VMEM),
        compiler_params=pltpu.CompilerParams(vmem_limit_bytes=4 * MIB),
        name="assemble",
    )(got)


def at(y, z, core):
    return y * 4 + z * 2 + core


SWAP_CORE = [(i, i ^ 1) for i in range(FRAMES)]
SAME_CORE = [[at(y, z, c) for y in range(8) for z in range(2)] for c in range(2)]
ALONG_X = [[z * 4 + x for x in range(4)] for z in range(4)]


def all_to_all(x, axis, groups=None):
    return lax.all_to_all(
        x, axis, split_axis=0, concat_axis=0, tiled=True, axis_index_groups=groups
    )


def swap_z(x, bits):
    return lax.ppermute(x, "clip", [(z * 4 + i, (z ^ bits) * 4 + i) for z in range(4) for i in range(4)])


def on_device(queries, keys, values, grad_out, w_out):
    weight = lax.all_gather(w_out, "frame", axis=0)
    clip = lax.axis_index("clip")
    place = jnp.stack([lax.axis_index("frame") & 1, clip & 3, clip >> 2])
    got = all_to_all(pack(queries, keys, values, grad_out), "frame")
    dy, attn, send, stats = forward(place, got, selection())

    other = lax.ppermute(send, "frame", SWAP_CORE)
    term, token = weight_term(attn, dy, other)
    out = backward(got, dy, stats, weight, token)
    term = add_x(all_to_all(term, "clip", ALONG_X))
    out = all_to_all(out, "frame")
    pair = term.astype(jnp.float32) + swap_z(term, 1).astype(jnp.float32)
    pair = pair.astype(jnp.bfloat16)
    term = add_z(pair, swap_z(pair, 3))

    out, term = lax.optimization_barrier((out, term))
    term = add_frames(all_to_all(term, "frame", SAME_CORE))
    grad_weight = assemble(all_to_all(term, "clip", ALONG_X))
    shape = (1, 1, TOKENS, WIDTH)
    return (
        out[:, 0].reshape(shape),
        out[:, 1].reshape(shape),
        out[:, 2].reshape(shape),
        grad_weight,
    )


def solution(mesh):
    spread = P("clip", "frame", None, None)
    return jax.shard_map(
        on_device,
        mesh=mesh,
        in_specs=(spread, spread, spread, spread, P("frame", None)),
        out_specs=(spread, spread, spread, P("frame", None)),
        check_vma=False,
    )
```
